32 devices in a mesh: samp: 8 (over y, x, core), var: 4 (over z).
Axes of the slice: x: 2, y: 2, z: 4, core: 2. Of those that a mesh axis runs over, the one named last changes fastest.
Arguments:
- genotypes: bfloat16 [8192, 16384], P('samp', 'var'), may hold values from 0 to 2, as said below
- col_mean: float32 [16384], P('var'), may hold values from 0.1 to 1, as said below
- inv_scale: float32 [16384], P('var'), may hold values from 1.4 to 3.25, as said below
- targets: float32 [8192], P('samp'), may hold values from -6 to 6
- probes: float32 [8192, 7], P('samp'), may hold values from -6 to 6
- delta: float32 [1], replicated, may hold values from 0.5 to 2
Outputs:
- solution: float32 [8192, 8], P('samp')
- assoc: float32 [16384], P('var')
The draws below stay inside these ranges and needn't reach their ends.
Inputs may be any that keep to these rules, and one draw needn't show every extreme that they name: `genotypes`: dosages 0, 1 or 2, drawn per variant from an allele frequency f of 0.05 to 0.5. `col_mean`: 2 f for the variant's allele frequency f. `inv_scale`: 1 / sqrt(2 f (1 - f)) for the same frequency f.
All inputs are finite; a program needn't handle non-finite values.
Results may differ from the reference program's by a relative error of at most 0.0003.
Values sent between devices are 32-bit elements; how exact they have to be, the bound alone decides.
No kernel may reach another device: no remote copies, remote signals or barrier semaphores. Data moves between devices by JAX's collectives and lax.ppermute only.
A program may use at most 64 MiB of HBM per device.

```python
import math
import jax
import jax.numpy as jnp
from jax import lax

M = 16384
COLS = 8
ITERS = 2
N = 8192


def allele_level(key):
    return jax.random.randint(jax.random.fold_in(key, 11), (M,), 50, 500)


def allele_freq(key):
    return allele_level(key).astype(jnp.float32) / 1000.0


def draw_genotypes(key, part):
    level = allele_level(key)
    values = jax.random.randint(jax.random.fold_in(key, 21), (N, M), 0, 1000000)
    first = (values % 1000 < level[None, :]).astype(jnp.float32)
    second = (values // 1000 < level[None, :]).astype(jnp.float32)
    return (first + second).astype(jnp.bfloat16)


def draw_col_mean(key, part):
    return 2.0 * allele_freq(key)


def draw_inv_scale(key, part):
    freq = allele_freq(key)
    return 1.0 / jnp.sqrt(2.0 * freq * (1.0 - freq))


def level_of(stream_key, shape, cuts, smallest, top_value):
    level = 1.0
    for axis_at, parts in cuts:
        steps = jax.random.uniform(jax.random.fold_in(jax.random.fold_in(stream_key, 6), axis_at), (parts,), jnp.float32, smallest / len(cuts), top_value / len(cuts))
        level = level * jnp.repeat(jnp.exp(steps), shape[axis_at] // parts).reshape((-1,) + (1,) * (len(shape) - 1 - axis_at))
    return level


def bell_draw(key, dims, width, reach, cuts=(), held_as=jnp.bfloat16):
    entries = width * jax.random.normal(key, dims, jnp.float32)
    if cuts:
        entries = entries * level_of(key, dims, cuts, -0.22, 0.18)
    return jnp.clip(entries, -reach, reach).astype(held_as)


def setup_inputs(seed: int = 0) -> dict:
    splits = jax.random.split(jax.random.key(seed), 7)
    genotypes = draw_genotypes(jax.random.fold_in(splits[6], 71), 0)
    col_mean = draw_col_mean(jax.random.fold_in(splits[6], 71), 0)
    inv_scale = draw_inv_scale(jax.random.fold_in(splits[6], 71), 0)
    targets = bell_draw(splits[3], (N,), 1.0, 6.0, ((0, 8),), jnp.float32)
    probes = bell_draw(splits[4], (N, COLS - 1), 1.0, 6.0, ((0, 8),), jnp.float32)
    delta = jnp.clip(jax.random.uniform(splits[5], (1,), jnp.float32, 0.5, 2.0), 0.5, 2.0)
    return {"genotypes": genotypes, "col_mean": col_mean, "inv_scale": inv_scale, "targets": targets, "probes": probes, "delta": delta}


HI = lax.Precision.HIGHEST

def blocks_of(genotypes):
    block = math.gcd(genotypes.shape[0], 512)
    return (genotypes.reshape(genotypes.shape[0] // block, block, genotypes.shape[1]), block)

def across(genotypes, col_mean, inv_scale, vectors):
    stacked, block = blocks_of(genotypes)
    pieces = vectors.reshape(stacked.shape[0], block, vectors.shape[1])

    def add_block(total, items):
        dense = items[0].astype(jnp.float32)
        return (total + lax.dot_general(dense, items[1], (((0,), (0,)), ((), ())), precision=HI, preferred_element_type=jnp.float32), None)
    start = jnp.zeros((genotypes.shape[1], vectors.shape[1]), jnp.float32)
    part, _ = lax.scan(add_block, start, (stacked, pieces))
    totals = lax.optimization_barrier(jnp.sum(vectors, 0))
    return inv_scale[:, None] * (part - col_mean[:, None] * totals[None, :])

def along(genotypes, col_mean, inv_scale, columns):
    stacked, block = blocks_of(genotypes)
    scaled = inv_scale[:, None] * columns
    offset = jnp.dot(col_mean, scaled, precision=HI, preferred_element_type=jnp.float32)
    rows = lax.map(lambda piece: jnp.dot(piece.astype(jnp.float32), scaled, precision=HI, preferred_element_type=jnp.float32), stacked)
    return rows.reshape(genotypes.shape[0], columns.shape[1]) - offset[None, :]

def reference(genotypes, col_mean, inv_scale, targets, probes, delta):
    shift = delta[0]
    rhs = jnp.concatenate([targets[:, None], probes], 1)
    solution = jnp.zeros_like(rhs)
    residual = rhs
    direction = rhs
    norm_now = lax.optimization_barrier(jnp.sum(residual * residual, 0))
    for step in range(ITERS):
        columns = across(genotypes, col_mean, inv_scale, direction)
        image = along(genotypes, col_mean, inv_scale, columns) / M + shift * direction
        alpha = norm_now / lax.optimization_barrier(jnp.sum(direction * image, 0))
        solution = solution + alpha[None, :] * direction
        residual = residual - alpha[None, :] * image
        norm_next = lax.optimization_barrier(jnp.sum(residual * residual, 0))
        direction = residual + (norm_next / norm_now)[None, :] * direction
        norm_now = norm_next
    first = across(genotypes, col_mean, inv_scale, solution[:, 0:1])[:, 0]
    assoc = first / jnp.sqrt(jnp.float32(N))
    return (solution, assoc)
```

```python
import functools

import jax
import jax.numpy as jnp
from jax import lax
from jax.experimental import pallas as pl
from jax.experimental.pallas import tpu as pltpu
from jax.sharding import PartitionSpec as P

LANES = 128
ROW_CHUNKS = 8
LIMIT = 40 << 20
F32 = jnp.float32
BF16 = jnp.bfloat16


def in_two(values):
    high = values.astype(BF16).astype(F32)
    return jnp.concatenate([high, values - high], 0).astype(BF16)


def summed(product):
    rows = product.shape[0] // 2
    return product[:rows] + product[rows:]


def tail_of(*columns):
    rows = columns[0].shape[0]
    lane = lax.broadcasted_iota(jnp.int32, (rows, LANES), 1)
    tail = jnp.zeros((rows, LANES), F32)
    for at, column in enumerate(columns):
        tail = jnp.where(lane == at, column, tail)
    return tail


def row_sum(values):
    return jnp.sum(values, 1, keepdims=True)


def put_halves(core, product, tail, own, other):
    half = product.shape[1] // 2

    def put(low, high):
        low[:, :half] = product[:, :half]
        high[:, :half] = product[:, half:]

    @pl.when(core == 0)
    def _():
        put(own, other)

    @pl.when(core == 1)
    def _():
        put(other, own)

    own[:, half:] = tail
    other[:, half:] = tail


def first_kernel(targets, probes, genotypes, held, rhs_out, own, other, sems):
    rows = genotypes.shape[0] // ROW_CHUNKS
    copies = [
        pltpu.make_async_copy(
            genotypes.at[pl.ds(at * rows, rows)], held.at[pl.ds(at * rows, rows)], sems.at[at]
        )
        for at in range(ROW_CHUNKS)
    ]
    for copy in copies:
        copy.start()
    rhs = jnp.concatenate([targets[...], probes[...]], 0)
    rhs_out[...] = rhs
    pieces = in_two(rhs)
    total = None
    for at, copy in enumerate(copies):
        copy.wait()
        part = jnp.dot(
            pieces[:, at * rows : (at + 1) * rows],
            held[pl.ds(at * rows, rows), :],
            preferred_element_type=F32,
        )
        total = part if total is None else total + part
    tail = tail_of(row_sum(rhs), row_sum(rhs * rhs))
    put_halves(lax.axis_index("samp") % 2, summed(total), tail, own, other)


def joined(own, mate):
    half = own.shape[1] - LANES
    core = lax.axis_index("samp") % 2
    mine, theirs = own[:, :half], mate[:, :half]
    low = jnp.where(core == 0, mine, theirs)
    high = jnp.where(core == 0, theirs, mine)
    return jnp.concatenate([low, high], 1)


def along_kernel(own, mate, col_mean, inv_scale, held, columns_out, part_out):
    half = own.shape[1] - LANES
    samples = held.shape[0]
    totals = own[:, half : half + 1]
    columns = inv_scale[...] * (joined(own, mate) - col_mean[...] * totals)
    columns_out[...] = columns
    scaled = inv_scale[...] * columns
    offset = row_sum(col_mean[...] * scaled)
    product = summed(
        lax.dot_general(
            in_two(scaled), held[...], (((1,), (1,)), ((), ())), preferred_element_type=F32
        )
    )
    part_out[:, :samples] = product - offset
    part_out[:, samples:] = tail_of(row_sum(columns * columns))


def second_kernel(m_total, delta, rhs, first, held, *rest):
    *parts, residual_out, alpha_out, own, other = rest
    samples = held.shape[0]
    image = functools.reduce(jnp.add, [part[...] for part in parts])
    half = first.shape[1] - LANES
    squares = first[:, half + 1 : half + 2]
    shift = delta[0]
    curving = image[:, samples : samples + 1] / m_total + shift * squares
    alpha = squares / curving
    direction = rhs[...]
    residual = direction - alpha * (image[:, :samples] / m_total + shift * direction)
    residual_out[...] = residual
    alpha_out[...] = jnp.broadcast_to(alpha, alpha_out.shape)
    product = summed(jnp.dot(in_two(residual), held[...], preferred_element_type=F32))
    tail = tail_of(
        row_sum(residual), row_sum(residual * residual), row_sum(residual * direction)
    )
    put_halves(lax.axis_index("samp") % 2, product, tail, own, other)


def third_kernel(own, mate, first, columns, col_mean, inv_scale, columns_out, part_out):
    half = own.shape[1] - LANES
    ratio = own[:, half + 1 : half + 2] / first[:, half + 1 : half + 2]
    fresh = inv_scale[...] * (joined(own, mate) - col_mean[...] * own[:, half : half + 1])
    fresh = fresh + ratio * columns[...]
    columns_out[...] = fresh[:1]
    part_out[...] = tail_of(row_sum(fresh * fresh))


def last_kernel(
    m_total, n_total, delta, rhs, residual, alpha, first, second, columns, fresh, *rest
):
    *parts, solution_out, assoc_out = rest
    half = first.shape[1] - LANES
    shift = delta[0]
    norm_first = first[:, half + 1 : half + 2]
    norm_now = second[:, half + 1 : half + 2]
    across = second[:, half + 2 : half + 3]
    ratio = norm_now / norm_first
    squares = norm_now + ratio * (2.0 * across + ratio * norm_first)
    column_squares = functools.reduce(jnp.add, [part[...] for part in parts])[:, :1]
    beta = norm_now / (column_squares / m_total + shift * squares)
    alpha = alpha[:, :1]
    direction = residual[...] + ratio * rhs[...]
    solution_out[...] = alpha * rhs[...] + beta * direction
    assoc_out[...] = (alpha[:1] * columns[:1, :] + beta[:1] * fresh[...]) / jnp.sqrt(
        jnp.float32(n_total)
    )


def per_device(genotypes, col_mean, inv_scale, targets, probes, delta):
    samples, variants = genotypes.shape
    samp, var = lax.axis_size("samp"), lax.axis_size("var")
    n_total, m_total = samples * samp, variants * var
    cols = probes.shape[1] + 1
    half = variants // 2

    vmem = pl.BlockSpec(memory_space=pltpu.VMEM)
    smem = pl.BlockSpec(memory_space=pltpu.SMEM)
    hbm = pl.BlockSpec(memory_space=pl.ANY)
    params = pltpu.CompilerParams(vmem_limit_bytes=LIMIT)

    def array(*shape):
        return jax.ShapeDtypeStruct(shape, F32)

    def swapped(values, axis, flip):
        size = lax.axis_size(axis)
        return lax.ppermute(values, axis, [(at, at ^ flip) for at in range(size)])

    def gathered(values, axis, first_bit):
        bit, size = first_bit, lax.axis_size(axis)
        while True:
            flips = [bit, 2 * bit, 3 * bit] if 2 * bit < size else [bit] * (bit < size)
            terms = [values] + [swapped(values, axis, flip) for flip in flips]
            bit *= 4
            if bit >= size:
                return terms
            values = functools.reduce(jnp.add, terms)

    def summed_over_samp(own, other):
        own = own + swapped(other, "samp", 1)
        return functools.reduce(jnp.add, gathered(own, "samp", 2))

    col_mean, inv_scale = col_mean[None, :], inv_scale[None, :]
    held, rhs, own, other = pl.pallas_call(
        first_kernel,
        in_specs=[vmem, vmem, hbm],
        out_specs=[vmem] * 4,
        out_shape=[
            pltpu.VMEM((samples, variants), BF16),
            array(cols, samples),
            array(cols, half + LANES),
            array(cols, half + LANES),
        ],
        scratch_shapes=[pltpu.SemaphoreType.DMA((ROW_CHUNKS,))],
        compiler_params=params,
        name="across_first",
    )(targets[None, :], probes.T, genotypes)
    held = pltpu.with_memory_space_constraint(held, pltpu.VMEM)
    first = summed_over_samp(own, other)
    mate = swapped(first, "samp", 1)
    columns, part = pl.pallas_call(
        along_kernel,
        in_specs=[vmem] * 5,
        out_specs=[vmem] * 2,
        out_shape=[array(cols, variants), array(cols, samples + LANES)],
        compiler_params=params,
        name="along",
    )(first, mate, col_mean, inv_scale, held)
    parts = gathered(part, "var", 1)
    residual, alpha, own, other = pl.pallas_call(
        functools.partial(second_kernel, m_total),
        in_specs=[smem] + [vmem] * (3 + len(parts)),
        out_specs=[vmem] * 4,
        out_shape=[
            array(cols, samples),
            array(cols, LANES),
            array(cols, half + LANES),
            array(cols, half + LANES),
        ],
        compiler_params=params,
        name="across_second",
    )(delta, rhs, first, held, *parts)
    second = summed_over_samp(own, other)
    mate = swapped(second, "samp", 1)
    fresh, part = pl.pallas_call(
        third_kernel,
        in_specs=[vmem] * 6,
        out_specs=[vmem] * 2,
        out_shape=[array(1, variants), array(cols, LANES)],
        compiler_params=params,
        name="columns",
    )(second, mate, first, columns, col_mean, inv_scale)
    parts = gathered(part, "var", 1)
    solved, assoc = pl.pallas_call(
        functools.partial(last_kernel, m_total, n_total),
        in_specs=[smem] + [vmem] * (7 + len(parts)),
        out_specs=[vmem] * 2,
        out_shape=[array(cols, samples), array(1, variants)],
        compiler_params=params,
        name="combine",
    )(delta, rhs, residual, alpha, first, second, columns, fresh, *parts)
    return (solved.T, assoc[0])


def solution(mesh):
    placed = (P("samp", "var"), P("var"), P("var"), P("samp"), P("samp", None), P())
    return jax.shard_map(
        per_device,
        mesh=mesh,
        in_specs=placed,
        out_specs=(P("samp", None), P("var")),
        check_vma=False,
    )
```
